512 devices in a mesh: pipe: 32 (over z, core), ulysses: 4 (over x), rep: 4 (over y).
Axes of the slice: x: 4, y: 4, z: 16, core: 2. Of those that a mesh axis runs over, the one named last changes fastest.
Arguments:
- latent: float32 [48, 32, 64], P('rep'), parts along dimension 0, may hold values from -6 to 6
- timesteps: int32 [8], P('rep'), parts along dimension 0, may hold values from 1 to 1000
- w_in: bfloat16 [64, 1536], replicated, may hold values from -0.75 to 0.75
- w_out: bfloat16 [1536, 64], replicated, may hold values from -0.15625 to 0.15625
- out_gain: float32 [1536], replicated, may hold values from 0.5 to 1.5
- w_qkv: bfloat16 [32, 1536, 12, 3, 128], P('pipe', None, 'ulysses'), may hold values from -0.15625 to 0.15625
- norm_gain: float32 [32, 1536], P('pipe'), may hold values from 0.5 to 1.5
- modulation: float32 [32, 1536], P('pipe'), may hold values from -3 to 3
- q_gain: float32 [32, 128], P('pipe'), may hold values from 0.5 to 1.5
- k_gain: float32 [32, 128], P('pipe'), may hold values from 0.5 to 1.5
Outputs:
- caches: bfloat16 [32, 2, 1536, 1536], P('pipe', None, 'rep', 'ulysses'), parts along dimension 2
The draws below stay inside these ranges and needn't reach their ends.
There are 4 independent parts, one for each index of `rep`. The reference program is written for one: setup_inputs(seed, part) draws one part's arguments, and reference() takes and returns one part's arrays. A program takes and returns all parts, laid end to end along the dimension named above; an argument that names none is the same for every part. Nothing has to cross between parts.
All inputs are finite; a program needn't handle non-finite values.
Results may differ from the reference program's by a relative error of at most 0.017.
Values may be sent and summed in bfloat16 or wider, within the bound.
A program may use at most 64 MiB of HBM per device.

```python
import jax
import jax.numpy as jnp
from jax import lax

D = 1536
HEADS = 12
HD = 128
C = 64
PATCHES = 12
STEPS = 2
PT = 32
TOKENS = 384
LAYERS = 32


def levels(own_key, extent, pieces, least, high):
    def one(axis_at, blocks):
        steps = jax.random.uniform(jax.random.fold_in(jax.random.fold_in(own_key, 6), axis_at), (blocks,), jnp.float32, least / len(pieces), high / len(pieces))
        return jnp.repeat(jnp.exp(steps), extent[axis_at] // blocks).reshape((-1,) + (1,) * (len(extent) - axis_at - 1))

    level = one(*pieces[0])
    for cut in pieces[1:]:
        level = level * one(*cut)
    return level


def noise(own_key, dims, spread, reach, pieces=(), kind=jnp.bfloat16):
    array = spread * jax.random.normal(own_key, dims, jnp.float32)
    if pieces:
        array = array * levels(own_key, dims, pieces, -0.22, 0.18)
    return jnp.clip(array, -reach, reach).astype(kind)


def setup_inputs(seed: int = 0, part: int = 0) -> dict:
    splits = jax.random.split(jax.random.key(seed), 11)
    part_keys = jax.random.split(jax.random.fold_in(splits[10], part), 11)
    latent = noise(part_keys[0], (PATCHES, PT, C), 1.0, 6.0, (), jnp.float32)
    timesteps = jax.random.randint(part_keys[1], (STEPS,), 1, 1001).astype(jnp.int32)
    w_in = noise(splits[2], (C, D), C ** -0.5, 0.75)
    w_out = noise(splits[3], (D, C), D ** -0.5, 0.15625)
    out_gain = jnp.clip(1.0 + 0.1 * jax.random.normal(splits[4], (D,), jnp.float32), 0.5, 1.5)
    w_qkv = noise(splits[5], (LAYERS, D, HEADS, 3, HD), D ** -0.5, 0.15625, ((0, 32), (2, 4)))
    norm_gain = jnp.clip(1.0 + 0.1 * jax.random.normal(splits[6], (LAYERS, D), jnp.float32), 0.5, 1.5)
    modulation = noise(splits[7], (LAYERS, D), 0.5, 3.0, ((0, 32),), jnp.float32)
    q_gain = jnp.clip(1.0 + 0.1 * jax.random.normal(splits[8], (LAYERS, HD), jnp.float32), 0.5, 1.5)
    k_gain = jnp.clip(1.0 + 0.1 * jax.random.normal(splits[9], (LAYERS, HD), jnp.float32), 0.5, 1.5)
    return dict(latent=latent, timesteps=timesteps, w_in=w_in, w_out=w_out, out_gain=out_gain, w_qkv=w_qkv, norm_gain=norm_gain, modulation=modulation, q_gain=q_gain, k_gain=k_gain)


EPS = 1e-06

def rms_scale(values):
    return values * lax.rsqrt(lax.optimization_barrier(jnp.mean(values * values, axis=-1, keepdims=True)) + EPS)

def head_norms(raw, q_scale, k_scale):
    query_rows = rms_scale(raw[:, :, 0]) * q_scale
    key = rms_scale(raw[:, :, 1]) * k_scale
    return jnp.stack([query_rows, key, raw[:, :, 2]], axis=2).astype(jnp.bfloat16)

def attend(query_rows, cached_key_rows, cached_value_rows, patch, step):
    score_scale = query_rows.shape[-1] ** (-0.5)
    attention_scores = jnp.einsum('qkj,fkj->kqf', query_rows.astype(jnp.float32), cached_key_rows.astype(jnp.float32)) * score_scale
    key_patch = jnp.arange(cached_key_rows.shape[0], dtype=jnp.int32) // PT
    allowed = (key_patch <= patch) | (step > 0)
    attention_scores = jnp.where(allowed[None, None, :], attention_scores, jnp.float32(-1e+30))
    softmax_weights = jnp.exp(attention_scores)
    softmax_weights = (softmax_weights / lax.optimization_barrier(jnp.sum(softmax_weights, axis=-1, keepdims=True))).astype(jnp.bfloat16)
    attended_values = jnp.einsum('bnf,fbv->nbv', softmax_weights.astype(jnp.float32), cached_value_rows.astype(jnp.float32))
    return attended_values.astype(jnp.bfloat16)

def reference(latent, timesteps, w_in, w_out, out_gain, w_qkv, norm_gain, modulation, q_gain, k_gain):
    sigma = timesteps.astype(jnp.float32) / 1000.0
    key_caches = jnp.zeros((LAYERS, TOKENS, HEADS, HD), jnp.bfloat16)
    value_caches = jnp.zeros((LAYERS, TOKENS, HEADS, HD), jnp.bfloat16)
    state = latent
    for step in range(STEPS):
        for patch in range(PATCHES):
            current = state[patch]
            hidden = jnp.dot(current.astype(jnp.bfloat16), w_in, preferred_element_type=jnp.float32)

            def layer(carry, inputs):
                weight, gain, shift, q_scale, k_scale, cached_key_rows, cached_value_rows = inputs
                normed = (rms_scale(carry) * gain * (1.0 + sigma[step] * shift)).astype(jnp.bfloat16)
                raw = jnp.einsum('rd,dhcn->rhcn', normed.astype(jnp.float32), weight.astype(jnp.float32))
                qkv = head_norms(raw, q_scale, k_scale)
                start = patch * PT
                cached_key_rows = lax.dynamic_update_slice_in_dim(cached_key_rows, qkv[:, :, 1], start, 0)
                cached_value_rows = lax.dynamic_update_slice_in_dim(cached_value_rows, qkv[:, :, 2], start, 0)
                attended_values = attend(qkv[:, :, 0], cached_key_rows, cached_value_rows, patch, step)
                carry = carry + attended_values.reshape(PT, HEADS * HD).astype(jnp.float32)
                return (carry, (cached_key_rows, cached_value_rows))
            hidden, (key_caches, value_caches) = lax.scan(layer, hidden, (w_qkv, norm_gain, modulation, q_gain, k_gain, key_caches, value_caches))
            if step < STEPS - 1:
                normed = (rms_scale(hidden) * out_gain).astype(jnp.bfloat16)
                velocity = jnp.dot(normed, w_out, preferred_element_type=jnp.float32)
                state = state.at[patch].set(current + (sigma[step + 1] - sigma[step]) * velocity)
    stacked = jnp.stack([key_caches, value_caches], axis=1)
    return stacked.reshape(LAYERS, 2, TOKENS, HEADS * HD)
```

```python
import functools

import jax
import jax.numpy as jnp
from jax import lax
from jax.experimental import pallas as pl
from jax.experimental.pallas import tpu as pltpu
from jax.sharding import PartitionSpec as P

EPS = 1e-06
BF = jnp.bfloat16
F32 = jnp.float32


def contract_last(a, b):
    return lax.dot_general(a, b, (((1,), (1,)), ((), ())), preferred_element_type=F32)


def pipeline(
    dims,
    ts_ref,
    latent_ref,
    w_in_ref,
    w_out_ref,
    out_gain_ref,
    norm_gain_ref,
    modulation_ref,
    q_gain_ref,
    k_gain_ref,
    w_hbm,
    caches_ref,
    w_ref,
    gains,
    arrived,
    arrived_low,
    sent,
    sent_low,
    w_sem,
    arrived_sem,
    arrived_low_sem,
    sent_sem,
    sent_low_sem,
):
    sections, groups, steps, patches, rows, heads, hd = dims
    jobs = steps * patches
    slab = heads * hd
    width = groups * slab
    tokens = patches * rows
    section = lax.axis_index("pipe")
    member = lax.axis_index("ulysses")
    following = lax.rem(section + 1, sections)
    preceding = lax.rem(section + sections - 1, sections)
    first = section == 0
    last = section == sections - 1
    wrap = jnp.where(last, patches, 0)

    def peer(distance):
        return lax.rem(member + distance, groups)

    def w_copy(kind, head):
        column = (kind * heads + head) * hd
        return pltpu.make_async_copy(
            w_hbm.at[0, head, (1, 0, 2)[kind]],
            w_ref.at[:, column : column + hd],
            w_sem.at[kind * heads + head],
        )

    for kind in range(3):
        for head in range(heads):
            w_copy(kind, head).start()

    barrier = pltpu.get_barrier_semaphore()
    for stage in (following, preceding):
        for distance in range(groups):
            pl.semaphore_signal(
                barrier,
                inc=1,
                device_id={"pipe": stage, "ulysses": peer(distance)},
                device_id_type=pl.DeviceIdType.MESH,
            )
    pl.semaphore_wait(barrier, 2 * groups)

    caches_ref[...] = jnp.zeros_like(caches_ref)
    for step in range(steps):
        sigma = jnp.full((1, width), ts_ref[step], jnp.int32).astype(F32) / 1000.0
        gain = norm_gain_ref[...] * (1.0 + sigma * modulation_ref[...])
        for part in range(groups):
            gains[step, part] = gain[:, part * slab : (part + 1) * slab]
    for kind in range(3):
        for head in range(heads):
            w_copy(kind, head).wait()

    def send(job, distance):
        return pltpu.make_async_remote_copy(
            src_ref=sent.at[job],
            dst_ref=arrived.at[job + wrap, member],
            send_sem=sent_sem.at[job, distance],
            recv_sem=arrived_sem.at[job + wrap, member],
            device_id={"pipe": following, "ulysses": peer(distance)},
            device_id_type=pl.DeviceIdType.MESH,
        )

    def send_low(job):
        return pltpu.make_async_remote_copy(
            src_ref=sent_low.at[job],
            dst_ref=arrived_low.at[job + wrap],
            send_sem=sent_low_sem.at[job],
            recv_sem=arrived_low_sem.at[job + wrap],
            device_id={"pipe": following},
            device_id_type=pl.DeviceIdType.MESH,
        )

    def receive(job, part):
        pltpu.make_async_remote_copy(
            src_ref=sent.at[job],
            dst_ref=arrived.at[job, part],
            send_sem=sent_sem.at[job, 0],
            recv_sem=arrived_sem.at[job, part],
            device_id={"pipe": preceding},
            device_id_type=pl.DeviceIdType.MESH,
        ).wait_recv()

    def receive_low(job):
        pltpu.make_async_remote_copy(
            src_ref=sent_low.at[job],
            dst_ref=arrived_low.at[job],
            send_sem=sent_low_sem.at[job],
            recv_sem=arrived_low_sem.at[job],
            device_id={"pipe": preceding},
            device_id_type=pl.DeviceIdType.MESH,
        ).wait_recv()

    near_to_far = sorted(range(groups), key=lambda d: min(d, groups - d))

    def embed(job, patch, state):
        state = state.astype(BF)
        for distance in near_to_far:
            part = peer(distance)
            columns = pl.ds(pl.multiple_of(part * slab, slab), slab)
            x = jnp.dot(state, w_in_ref[:, columns], preferred_element_type=F32)
            high = x.astype(BF)
            arrived[job, part] = high
            if distance == 0:
                arrived_low[job] = (x - high.astype(F32)).astype(BF)

    def next_state(job, step, patch):
        square = jnp.zeros((rows, hd), F32)
        for part in range(groups):
            receive(job, part)
            x = arrived[job, part].astype(F32)
            for head in range(heads):
                piece = x[:, head * hd : (head + 1) * hd]
                square += piece * piece
        receive_low(job)
        scale = lax.rsqrt(jnp.sum(square, axis=-1, keepdims=True) / width + EPS)
        velocity = jnp.zeros((rows, latent_ref.shape[2]), F32)
        for part in range(groups):
            columns = slice(part * slab, (part + 1) * slab)
            normed = arrived[job, part].astype(F32) * scale * out_gain_ref[:, columns]
            velocity += contract_last(normed.astype(BF), w_out_ref[:, columns])
        sigma = [
            jnp.full((1, velocity.shape[1]), ts_ref[at], jnp.int32).astype(F32) / 1000.0
            for at in (0, 1)
        ]
        return latent_ref[patch] + (sigma[1] - sigma[0]) * velocity

    def run(job, _):
        step = job // patches
        patch = job - step * patches

        @pl.when(first & (step == 0))
        def _():
            embed(job, patch, latent_ref[patch])

        @pl.when(first & (step > 0))
        def _():
            embed(job, patch, next_state(job, step, patch))

        square = jnp.zeros((rows, hd), F32)
        raw = None
        for distance in near_to_far:
            part = peer(distance)

            @pl.when(jnp.logical_not(first))
            def _():
                receive(job, part)

            x = arrived[job, part].astype(F32)
            for head in range(heads):
                piece = x[:, head * hd : (head + 1) * hd]
                square += piece * piece
            h = (x * gains[step, part]).astype(BF)
            depth = pl.ds(pl.multiple_of(part * slab, slab), slab)
            term = jnp.dot(h, w_ref[depth, :], preferred_element_type=F32)
            raw = term if raw is None else raw + term
        mean_square = jnp.sum(square, axis=-1, keepdims=True) / width
        scale = lax.rsqrt(mean_square + EPS)
        eps = EPS * (mean_square + EPS)

        def of(kind, head):
            column = (kind * heads + head) * hd
            return raw[:, column : column + hd]

        def head_scale(value):
            return lax.rsqrt(jnp.mean(value * value, axis=-1, keepdims=True) + eps)

        here = pl.ds(pl.multiple_of(patch * rows, rows), rows)
        for head in range(heads):
            columns = slice(head * hd, (head + 1) * hd)
            key = of(0, head)
            key = key * head_scale(key) * k_gain_ref[...]
            caches_ref[0, 0, here, columns] = key.astype(BF)
        for head in range(heads):
            columns = slice(head * hd, (head + 1) * hd)
            caches_ref[0, 1, here, columns] = (of(2, head) * scale).astype(BF)
        limit = jnp.where(step == 0, (patch + 1) * rows, tokens)
        allowed = lax.broadcasted_iota(jnp.int32, (rows, tokens), 1) < limit
        weights = []
        for head in range(heads):
            columns = slice(head * hd, (head + 1) * hd)
            query = of(1, head)
            scores = contract_last(
                (query * q_gain_ref[...]).astype(BF), caches_ref[0, 0, :, columns]
            )
            scores = scores * (head_scale(query) * (hd**-0.5))
            weights.append(jnp.where(allowed, jnp.exp(scores), 0.0))

        @pl.when(jnp.logical_not(first))
        def _():
            receive_low(job)

        for head in range(heads):
            columns = slice(head * hd, (head + 1) * hd)
            total = jnp.sum(weights[head], axis=-1, keepdims=True)
            attended = jnp.dot(
                weights[head].astype(BF),
                caches_ref[0, 1, :, columns],
                preferred_element_type=F32,
            )
            attended = (attended / total).astype(BF).astype(F32)
            x = arrived[job, member, :, columns].astype(F32)
            x = x + arrived_low[job, :, columns].astype(F32) + attended
            high = x.astype(BF)
            sent[job, :, columns] = high
            sent_low[job, :, columns] = (x - high.astype(F32)).astype(BF)

        @pl.when(jnp.logical_not(last) | (step < steps - 1))
        def _():
            for distance in near_to_far[::-1]:
                send(job, distance).start()
            send_low(job).start()

        return 0

    lax.fori_loop(0, jobs, run, 0)

    def finish(job, _):
        @pl.when(jnp.logical_not(last) | (job < jobs - patches))
        def _():
            for distance in range(groups):
                send(job, distance).wait_send()
            send_low(job).wait_send()

        return 0

    lax.fori_loop(0, jobs, finish, 0)


def shards(latent, timesteps, w_in, w_out, out_gain, w_qkv, norm_gain, modulation, q_gain, k_gain):
    sections = lax.axis_size("pipe")
    groups = lax.axis_size("ulysses")
    patches, rows, channels = latent.shape
    steps = timesteps.shape[0]
    width = w_in.shape[1]
    heads, hd = w_qkv.shape[2], w_qkv.shape[4]
    jobs = steps * patches
    slab = heads * hd
    tokens = patches * rows
    vmem = pl.BlockSpec(memory_space=pltpu.VMEM)
    dma = pltpu.SemaphoreType.DMA
    return pl.pallas_call(
        functools.partial(pipeline, (sections, groups, steps, patches, rows, heads, hd)),
        out_shape=jax.ShapeDtypeStruct((1, 2, tokens, slab), BF),
        in_specs=[pl.BlockSpec(memory_space=pltpu.SMEM)]
        + [vmem] * 8
        + [pl.BlockSpec(memory_space=pl.ANY)],
        out_specs=vmem,
        scratch_shapes=[
            pltpu.VMEM((width, 3 * slab), BF),
            pltpu.VMEM((steps, groups, 1, slab), F32),
            pltpu.VMEM((jobs, groups, rows, slab), BF),
            pltpu.VMEM((jobs, rows, slab), BF),
            pltpu.VMEM((jobs, rows, slab), BF),
            pltpu.VMEM((jobs, rows, slab), BF),
            dma((3 * heads,)),
            dma((jobs, groups)),
            dma((jobs,)),
            dma((jobs, groups)),
            dma((jobs,)),
        ],
        compiler_params=pltpu.CompilerParams(
            collective_id=0, has_side_effects=True, vmem_limit_bytes=32 << 20
        ),
        name="pipeline",
    )(
        timesteps,
        latent,
        w_in,
        w_out.T,
        out_gain.reshape(1, width),
        norm_gain,
        modulation,
        q_gain,
        k_gain,
        jnp.transpose(w_qkv, (0, 2, 3, 1, 4)),
    )


def solution(mesh):
    placed = (
        P("rep", None, None),
        P("rep"),
        P(),
        P(),
        P(),
        P("pipe", None, "ulysses", None, None),
        P("pipe", None),
        P("pipe", None),
        P("pipe", None),
        P("pipe", None),
    )
    return jax.shard_map(
        shards,
        mesh=mesh,
        in_specs=placed,
        out_specs=P("pipe", None, "rep", "ulysses"),
        check_vma=False,
    )
```

```python
import functools

import jax
import jax.numpy as jnp
from jax import lax
from jax.experimental import pallas as pl
from jax.experimental.pallas import tpu as pltpu
from jax.sharding import PartitionSpec as P

EPS = 1e-06
BF = jnp.bfloat16
F32 = jnp.float32


def contract_last(a, b):
    return lax.dot_general(a, b, (((1,), (1,)), ((), ())), preferred_element_type=F32)


def pipeline(
    dims,
    ts_ref,
    latent_hbm,
    w_in_hbm,
    w_out_hbm,
    out_gain_hbm,
    norm_gain_hbm,
    modulation_hbm,
    q_gain_hbm,
    k_gain_hbm,
    w_hbm,
    out_hbm,
    latent_ref,
    w_in_ref,
    w_out_ref,
    out_gain_ref,
    norm_gain_ref,
    modulation_ref,
    q_gain_ref,
    k_gain_ref,
    w_ref,
    gains,
    caches_ref,
    embedded,
    embedded_low,
    arrived,
    arrived_low,
    kept,
    sent,
    sent_low,
    edge_sem,
    w_sem,
    moved_sem,
    arrived_sem,
    low_sem,
    sent_sem,
    sent_low_sem,
    caches_sem,
    out_sem,
):
    sections, groups, steps, patches, rows, heads, hd = dims
    jobs = steps * patches
    slab = heads * hd
    width = groups * slab
    tokens = patches * rows
    section = lax.axis_index("pipe")
    member = lax.axis_index("ulysses")
    worker = lax.rem(section, 2) == 1
    helper = lax.rem(section, 2) == 0
    first = section < 2
    last = section >= sections - 2
    edge = section == 0
    following = lax.rem(section + 2, sections)
    preceding = lax.rem(section + sections - 2, sections)
    onward = jnp.where(last, 0, following)
    mesh_id = pl.DeviceIdType.MESH

    def peer(distance):
        return lax.rem(member + distance, groups)

    def greet(stage, distances):
        for distance in distances:
            pl.semaphore_signal(
                pltpu.get_barrier_semaphore(),
                inc=1,
                device_id={"pipe": stage, "ulysses": peer(distance)},
                device_id_type=mesh_id,
            )

    everyone = range(groups)

    @pl.when(helper)
    def _():
        greet(section + 1, [0])

    @pl.when(edge)
    def _():
        greet(sections - 1, everyone)

    @pl.when(worker)
    def _():
        greet(section - 1, [0])
        greet(section, everyone[1:])

    @pl.when(worker & jnp.logical_not(first))
    def _():
        greet(preceding, everyone)

    @pl.when(worker & jnp.logical_not(last))
    def _():
        greet(following, everyone)

    @pl.when(worker & last)
    def _():
        greet(0, everyone)

    met = jnp.where(
        worker,
        groups + jnp.where(first, 0, groups) + groups,
        jnp.where(edge, 1 + groups, 1),
    )

    distances = sorted(everyone, key=lambda d: min(d, groups - d))
    seen_as = {d: distances.index((groups - d) % groups) for d in everyone}

    def columns_of(at):
        return pl.ds(pl.multiple_of(peer(distances[at]) * slab, slab), slab)

    pieces = [
        (norm_gain_hbm, norm_gain_ref),
        (modulation_hbm, modulation_ref),
        (q_gain_hbm, q_gain_ref),
        (k_gain_hbm, k_gain_ref),
    ]

    def parameter(block, at):
        if at < 4:
            return pieces[at][0], pieces[at][1].at[block]
        owner, matrix = divmod(at - 4, 3 * heads)
        kind, head = divmod(matrix, heads)
        column = matrix * hd
        return (
            w_hbm.at[0, head, (1, 0, 2)[kind], columns_of(owner)],
            w_ref.at[block, owner * slab : (owner + 1) * slab, column : column + hd],
        )

    parameters = range(4 + 3 * heads * groups)

    def load(at):
        return pltpu.make_async_copy(*parameter(1, at), w_sem.at[1, at])

    def hand(at):
        source, target = parameter(0, at)
        return pltpu.make_async_remote_copy(
            src_ref=source,
            dst_ref=target,
            send_sem=moved_sem.at[at],
            recv_sem=w_sem.at[0, at],
            device_id={"pipe": section + 1},
            device_id_type=mesh_id,
        )

    def handed(at):
        source, target = parameter(0, at)
        return pltpu.make_async_copy(source, target, w_sem.at[0, at])

    def hand_back():
        return pltpu.make_async_remote_copy(
            src_ref=caches_ref.at[0],
            dst_ref=caches_ref.at[0],
            send_sem=caches_sem.at[0],
            recv_sem=caches_sem.at[1],
            device_id={"pipe": section - 1},
            device_id_type=mesh_id,
        )

    def receive(block, job, at):
        return pltpu.make_async_copy(
            sent.at[block, job], arrived.at[block, job, at], arrived_sem.at[block, job, at]
        )

    def receive_low(job):
        return pltpu.make_async_copy(sent_low.at[job], arrived_low.at[job], low_sem.at[job])

    @pl.when(helper)
    def _():
        first_only = [
            pltpu.make_async_copy(*pair, edge_sem.at[i])
            for i, pair in enumerate(
                [
                    (latent_hbm, latent_ref),
                    (w_in_hbm, w_in_ref),
                    (w_out_hbm, w_out_ref),
                    (out_gain_hbm, out_gain_ref),
                ]
            )
        ]

        @pl.when(edge)
        def _():
            for copy in first_only:
                copy.start()

        pl.semaphore_wait(pltpu.get_barrier_semaphore(), met)
        for at in parameters:
            hand(at).start()

        def hand_slab(job, at):
            return pltpu.make_async_remote_copy(
                src_ref=embedded.at[job, at],
                dst_ref=arrived.at[0, job, at],
                send_sem=sent_sem.at[0, job, at],
                recv_sem=arrived_sem.at[0, job, at],
                device_id={"pipe": section + 1},
                device_id_type=mesh_id,
            )

        def hand_low(job):
            return pltpu.make_async_remote_copy(
                src_ref=embedded_low.at[job],
                dst_ref=arrived_low.at[job],
                send_sem=sent_low_sem.at[job],
                recv_sem=low_sem.at[job],
                device_id={"pipe": section + 1},
                device_id_type=mesh_id,
            )

        def embed(job, state):
            state = state.astype(BF)
            for at in everyone:
                x = jnp.dot(state, w_in_ref[:, columns_of(at)], preferred_element_type=F32)
                high = x.astype(BF)
                embedded[job, at] = high
                if at == 0:
                    embedded_low[job] = (x - high.astype(F32)).astype(BF)
            for at in everyone:
                hand_slab(job, at).start()
            hand_low(job).start()

        def next_state(patch):
            square = jnp.zeros((rows, hd), F32)
            for at in everyone:
                receive(0, patch, at).wait()
            final = [arrived[0, patch, at].astype(F32) for at in everyone]
            for x in final:
                for head in range(heads):
                    piece = x[:, head * hd : (head + 1) * hd]
                    square += piece * piece
            scale = lax.rsqrt(jnp.sum(square, axis=-1, keepdims=True) / width + EPS)
            velocity = jnp.zeros((rows, latent_ref.shape[2]), F32)
            for at in everyone:
                normed = final[at] * scale * out_gain_ref[:, columns_of(at)]
                velocity += contract_last(normed.astype(BF), w_out_ref[:, columns_of(at)])
            sigma = [
                jnp.full((1, velocity.shape[1]), ts_ref[at], jnp.int32).astype(F32) / 1000.0
                for at in (0, 1)
            ]
            return latent_ref[patch] + (sigma[1] - sigma[0]) * velocity

        @pl.when(edge)
        def _():
            for copy in first_only:
                copy.wait()

            def start(patch, _):
                embed(patch, latent_ref[patch])
                return 0

            def again(patch, _):
                embed(patches + patch, next_state(patch))
                return 0

            def finish(job, _):
                for at in everyone:
                    hand_slab(job, at).wait_send()
                hand_low(job).wait_send()
                return 0

            lax.fori_loop(0, patches, start, 0)
            lax.fori_loop(0, patches, again, 0)
            lax.fori_loop(0, jobs, finish, 0)

        for at in parameters:
            hand(at).wait_send()
        pltpu.make_async_copy(caches_ref.at[0], caches_ref.at[0], caches_sem.at[1]).wait()
        out = pltpu.make_async_copy(caches_ref.at[0], out_hbm.at[0], out_sem)
        out.start()
        out.wait()

    @pl.when(worker)
    def _():
        for at in parameters:
            load(at).start()
        caches_ref[...] = jnp.zeros_like(caches_ref)
        pl.semaphore_wait(pltpu.get_barrier_semaphore(), met)
        for block, copy in ((0, handed), (1, load)):
            for at in range(4):
                copy(at).wait()
            for step in range(steps):
                sigma = jnp.full((1, slab), ts_ref[step], jnp.int32).astype(F32) / 1000.0
                for at in everyone:
                    gain = norm_gain_ref[block, :, columns_of(at)]
                    shift = modulation_ref[block, :, columns_of(at)]
                    gains[block, step, :, at * slab : (at + 1) * slab] = gain * (1.0 + sigma * shift)
            for at in parameters[4:]:
                copy(at).wait()

        def send(block, job, distance):
            at = seen_as[distance]
            return pltpu.make_async_remote_copy(
                src_ref=sent.at[block, job],
                dst_ref=arrived.at[1 - block, job, at],
                send_sem=sent_sem.at[block, job, distance],
                recv_sem=arrived_sem.at[1 - block, job, at],
                device_id={
                    "pipe": onward if block else section,
                    "ulysses": peer(distance),
                },
                device_id_type=mesh_id,
            )

        def send_low(job):
            return pltpu.make_async_remote_copy(
                src_ref=sent_low.at[job],
                dst_ref=arrived_low.at[job],
                send_sem=sent_low_sem.at[job],
                recv_sem=low_sem.at[job],
                device_id={"pipe": onward},
                device_id_type=mesh_id,
            )

        def run(block, step, patch):
            job = step * patches + patch
            gain = gains[block, step]
            square = jnp.zeros((rows, hd), F32)
            raw = None
            for at in everyone:
                if at or block == 0:
                    receive(block, job, at).wait()
                    x = arrived[block, job, at].astype(F32)
                else:
                    x = kept[patch]
                for head in range(heads):
                    piece = x[:, head * hd : (head + 1) * hd]
                    square += piece * piece
                x = (x * gain[:, at * slab : (at + 1) * slab]).astype(BF)
                term = jnp.dot(
                    x, w_ref[block, at * slab : (at + 1) * slab, :], preferred_element_type=F32
                )
                raw = term if raw is None else raw + term
            mean_square = jnp.sum(square, axis=-1, keepdims=True) / width
            scale = lax.rsqrt(mean_square + EPS)
            eps = EPS * (mean_square + EPS)

            def of(kind, head):
                column = (kind * heads + head) * hd
                return raw[:, column : column + hd]

            def head_scale(value):
                return lax.rsqrt(jnp.mean(value * value, axis=-1, keepdims=True) + eps)

            here = pl.ds(pl.multiple_of(patch * rows, rows), rows)
            for head in range(heads):
                columns = slice(head * hd, (head + 1) * hd)
                key = of(0, head)
                key = key * head_scale(key) * k_gain_ref[block]
                caches_ref[block, 0, here, columns] = key.astype(BF)
            for head in range(heads):
                columns = slice(head * hd, (head + 1) * hd)
                caches_ref[block, 1, here, columns] = (of(2, head) * scale).astype(BF)
            limit = jnp.where(step == 0, (patch + 1) * rows, tokens)
            allowed = lax.broadcasted_iota(jnp.int32, (rows, tokens), 1) < limit
            weights = []
            for head in range(heads):
                columns = slice(head * hd, (head + 1) * hd)
                query = of(1, head)
                scores = contract_last(
                    (query * q_gain_ref[block]).astype(BF), caches_ref[block, 0, :, columns]
                )
                scores = scores * (head_scale(query) * (hd**-0.5))
                weights.append(jnp.where(allowed, jnp.exp(scores), 0.0))
            if block == 0:
                receive_low(job).wait()
            for head in range(heads):
                columns = slice(head * hd, (head + 1) * hd)
                total = jnp.sum(weights[head], axis=-1, keepdims=True)
                attended = jnp.dot(
                    weights[head].astype(BF),
                    caches_ref[block, 1, :, columns],
                    preferred_element_type=F32,
                )
                attended = (attended / total).astype(BF).astype(F32)
                if block == 0:
                    x = arrived[0, job, 0, :, columns].astype(F32)
                    x = x + arrived_low[job, :, columns].astype(F32) + attended
                    kept[patch, :, columns] = x
                    sent[0, job, :, columns] = x.astype(BF)
                else:
                    x = kept[patch, :, columns] + attended
                    high = x.astype(BF)
                    sent[1, job, :, columns] = high
                    sent_low[job, :, columns] = (x - high.astype(F32)).astype(BF)

            if block == 0:
                for distance in distances[:0:-1]:
                    send(0, job, distance).start()
            else:

                @pl.when(jnp.logical_not(last) | (step < steps - 1))
                def _():
                    for distance in distances[::-1]:
                        send(1, job, distance).start()

                @pl.when(jnp.logical_not(last))
                def _():
                    send_low(job).start()

        turns = patches + 1

        def turn(at, _):
            step = at // turns
            patch = at - step * turns

            @pl.when(patch < patches)
            def _():
                run(0, step, patch)

            @pl.when(at == steps * turns - 1)
            def _():
                hand_back().start()

            @pl.when(patch > 0)
            def _():
                run(1, step, patch - 1)

            return 0

        lax.fori_loop(0, steps * turns, turn, 0)
        out = pltpu.make_async_copy(caches_ref.at[1], out_hbm.at[0], out_sem)
        out.start()

        def finish(job, _):
            for distance in distances[1:]:
                send(0, job, distance).wait_send()

            @pl.when(jnp.logical_not(last) | (job < jobs - patches))
            def _():
                for distance in everyone:
                    send(1, job, distance).wait_send()

            @pl.when(jnp.logical_not(last))
            def _():
                send_low(job).wait_send()

            return 0

        lax.fori_loop(0, jobs, finish, 0)
        hand_back().wait_send()
        out.wait()


def shards(latent, timesteps, w_in, w_out, out_gain, w_qkv, norm_gain, modulation, q_gain, k_gain):
    sections = lax.axis_size("pipe")
    groups = lax.axis_size("ulysses")
    patches, rows, channels = latent.shape
    steps = timesteps.shape[0]
    width = w_in.shape[1]
    heads, hd = w_qkv.shape[2], w_qkv.shape[4]
    jobs = steps * patches
    slab = heads * hd
    tokens = patches * rows
    dma = pltpu.SemaphoreType.DMA
    parameters = 4 + 3 * heads * groups
    return pl.pallas_call(
        functools.partial(pipeline, (sections, groups, steps, patches, rows, heads, hd)),
        out_shape=jax.ShapeDtypeStruct((1, 2, tokens, slab), BF),
        in_specs=[pl.BlockSpec(memory_space=pltpu.SMEM)] + [pl.BlockSpec(memory_space=pl.ANY)] * 9,
        out_specs=pl.BlockSpec(memory_space=pl.ANY),
        scratch_shapes=[
            pltpu.VMEM((patches, rows, channels), F32),
            pltpu.VMEM((channels, width), BF),
            pltpu.VMEM((channels, width), BF),
            pltpu.VMEM((1, width), F32),
            pltpu.VMEM((2, 1, width), F32),
            pltpu.VMEM((2, 1, width), F32),
            pltpu.VMEM((2, 1, hd), F32),
            pltpu.VMEM((2, 1, hd), F32),
            pltpu.VMEM((2, width, 3 * slab), BF),
            pltpu.VMEM((2, steps, 1, width), F32),
            pltpu.VMEM((2, 2, tokens, slab), BF),
            pltpu.VMEM((jobs, groups, rows, slab), BF),
            pltpu.VMEM((jobs, rows, slab), BF),
            pltpu.VMEM((2, jobs, groups, rows, slab), BF),
            pltpu.VMEM((jobs, rows, slab), BF),
            pltpu.VMEM((patches, rows, slab), F32),
            pltpu.VMEM((2, jobs, rows, slab), BF),
            pltpu.VMEM((jobs, rows, slab), BF),
            dma((4,)),
            dma((2, parameters)),
            dma((parameters,)),
            dma((2, jobs, groups)),
            dma((jobs,)),
            dma((2, jobs, groups)),
            dma((jobs,)),
            dma((2,)),
            dma,
        ],
        compiler_params=pltpu.CompilerParams(
            collective_id=0, has_side_effects=True, vmem_limit_bytes=60 << 20
        ),
        name="pipeline",
    )(
        timesteps,
        latent,
        w_in,
        w_out.T,
        out_gain.reshape(1, width),
        norm_gain,
        modulation,
        q_gain,
        k_gain,
        jnp.transpose(w_qkv, (0, 2, 3, 1, 4)),
    )


def solution(mesh):
    placed = (
        P("rep", None, None),
        P("rep"),
        P(),
        P(),
        P(),
        P("pipe", None, "ulysses", None, None),
        P("pipe", None),
        P("pipe", None),
        P("pipe", None),
        P("pipe", None),
    )
    return jax.shard_map(
        shards,
        mesh=mesh,
        in_specs=placed,
        out_specs=P("pipe", None, "rep", "ulysses"),
        check_vma=False,
    )
```

```python
import functools

import jax
import jax.numpy as jnp
from jax import lax
from jax.experimental import pallas as pl
from jax.experimental.pallas import tpu as pltpu
from jax.sharding import PartitionSpec as P

EPS = 1e-06
BF = jnp.bfloat16
F32 = jnp.float32


def contract_last(a, b):
    return lax.dot_general(a, b, (((1,), (1,)), ((), ())), preferred_element_type=F32)


def pipeline(
    dims,
    ts_ref,
    latent_hbm,
    w_in_hbm,
    w_out_hbm,
    out_gain_hbm,
    norm_gain_hbm,
    modulation_hbm,
    q_gain_hbm,
    k_gain_hbm,
    w_hbm,
    out_hbm,
    latent_ref,
    w_in_ref,
    w_out_ref,
    out_gain_ref,
    norm_gain_ref,
    modulation_ref,
    q_gain_ref,
    k_gain_ref,
    w_ref,
    gains,
    caches_ref,
    arrived,
    arrived_low,
    kept,
    sent,
    sent_low,
    edge_sem,
    w_sem,
    moved_sem,
    arrived_sem,
    low_sem,
    sent_sem,
    sent_low_sem,
    caches_sem,
    out_sem,
):
    sections, groups, steps, patches, rows, heads, hd = dims
    jobs = steps * patches
    slab = heads * hd
    width = groups * slab
    tokens = patches * rows
    section = lax.axis_index("pipe")
    member = lax.axis_index("ulysses")
    worker = lax.rem(section, 2) == 1
    helper = lax.rem(section, 2) == 0
    first = section < 2
    last = section >= sections - 2
    edge = section == 0
    following = lax.rem(section + 2, sections)
    preceding = lax.rem(section + sections - 2, sections)
    onward = jnp.where(last, 0, following)
    mesh_id = pl.DeviceIdType.MESH

    def peer(distance):
        return lax.rem(member + distance, groups)

    def greet(stage, distances):
        for distance in distances:
            pl.semaphore_signal(
                pltpu.get_barrier_semaphore(),
                inc=1,
                device_id={"pipe": stage, "ulysses": peer(distance)},
                device_id_type=mesh_id,
            )

    everyone = range(groups)

    @pl.when(helper & jnp.logical_not(edge))
    def _():
        greet(section + 1, [0])

    @pl.when(edge)
    def _():
        greet(sections - 1, everyone)
        greet(1, everyone)

    @pl.when(worker & first)
    def _():
        greet(0, everyone)

    @pl.when(worker & jnp.logical_not(first))
    def _():
        greet(section - 1, [0])
        greet(section, everyone[1:])
        greet(preceding, everyone)

    @pl.when(worker)
    def _():
        greet(onward, everyone)

    met = jnp.where(
        worker, jnp.where(first, 2 * groups, 3 * groups), jnp.where(edge, 2 * groups, 1)
    )
    leads = edge | (worker & jnp.logical_not(first))

    distances = sorted(everyone, key=lambda d: (min(d, groups - d), -d))
    seen_as = {d: distances.index((groups - d) % groups) for d in everyone}

    def columns_of(at):
        return pl.ds(pl.multiple_of(peer(distances[at]) * slab, slab), slab)

    pieces = [
        (norm_gain_hbm, norm_gain_ref),
        (modulation_hbm, modulation_ref),
        (q_gain_hbm, q_gain_ref),
        (k_gain_hbm, k_gain_ref),
    ]

    def parameter(block, at):
        if at < 4:
            return pieces[at][0], pieces[at][1].at[block]
        owner, matrix = divmod(at - 4, 3 * heads)
        kind, head = divmod(matrix, heads)
        column = matrix * hd
        return (
            w_hbm.at[0, head, (1, 0, 2)[kind], columns_of(owner)],
            w_ref.at[block, owner * slab : (owner + 1) * slab, column : column + hd],
        )

    parameters = range(4 + 3 * heads * groups)

    def load(at):
        return pltpu.make_async_copy(*parameter(1, at), w_sem.at[1, at])

    def hand(at):
        source, target = parameter(0, at)
        return pltpu.make_async_remote_copy(
            src_ref=source,
            dst_ref=target,
            send_sem=moved_sem.at[at],
            recv_sem=w_sem.at[0, at],
            device_id={"pipe": section + 1},
            device_id_type=mesh_id,
        )

    def handed(at):
        source, target = parameter(0, at)
        return pltpu.make_async_copy(source, target, w_sem.at[0, at])

    def hand_back():
        return pltpu.make_async_remote_copy(
            src_ref=caches_ref.at[0],
            dst_ref=caches_ref.at[0],
            send_sem=caches_sem.at[0],
            recv_sem=caches_sem.at[1],
            device_id={"pipe": section - 1},
            device_id_type=mesh_id,
        )

    def receive(block, job, at):
        slot = arrived.at[block, job, at]
        return pltpu.make_async_copy(slot, slot, arrived_sem.at[block, job, at])

    def receive_low(job):
        return pltpu.make_async_copy(sent_low.at[job], arrived_low.at[job], low_sem.at[job])

    @pl.when(helper & jnp.logical_not(edge))
    def _():
        pl.semaphore_wait(pltpu.get_barrier_semaphore(), met)
        for at in parameters:
            hand(at).start()
        for at in parameters:
            hand(at).wait_send()
        pltpu.make_async_copy(caches_ref.at[0], caches_ref.at[0], caches_sem.at[1]).wait()
        out = pltpu.make_async_copy(caches_ref.at[0], out_hbm.at[0], out_sem)
        out.start()
        out.wait()

    @pl.when(worker | edge)
    def _():
        first_only = [
            pltpu.make_async_copy(*pair, edge_sem.at[i])
            for i, pair in enumerate(
                [
                    (latent_hbm, latent_ref),
                    (w_in_hbm, w_in_ref),
                    (w_out_hbm, w_out_ref),
                    (out_gain_hbm, out_gain_ref),
                ]
            )
        ]

        @pl.when(edge)
        def _():
            for copy in first_only:
                copy.start()
            for at in parameters:
                handed(at).start()

        @pl.when(worker)
        def _():
            for at in parameters:
                load(at).start()

        caches_ref[...] = jnp.zeros_like(caches_ref)
        pl.semaphore_wait(pltpu.get_barrier_semaphore(), met)

        def prepare(block, copy):
            for at in range(4):
                copy(at).wait()
            for step in range(steps):
                sigma = jnp.full((1, slab), ts_ref[step], jnp.int32).astype(F32) / 1000.0
                for at in everyone:
                    gain = norm_gain_ref[block, :, columns_of(at)]
                    shift = modulation_ref[block, :, columns_of(at)]
                    gains[block, step, :, at * slab : (at + 1) * slab] = gain * (1.0 + sigma * shift)
            for at in parameters[4:]:
                copy(at).wait()

        @pl.when(edge)
        def _():
            for copy in first_only:
                copy.wait()

        @pl.when(leads)
        def _():
            prepare(0, handed)

        @pl.when(worker)
        def _():
            prepare(1, load)

        def embed(job, state):
            state = state.astype(BF)
            for at in everyone:
                x = jnp.dot(state, w_in_ref[:, columns_of(at)], preferred_element_type=F32)
                high = x.astype(BF)
                arrived[0, job, at] = high
                if at == 0:
                    arrived_low[job] = (x - high.astype(F32)).astype(BF)

        def next_state(patch):
            square = jnp.zeros((rows, hd), F32)
            for at in everyone:
                receive(0, jobs + patch, at).wait()
            final = [arrived[0, jobs + patch, at].astype(F32) for at in everyone]
            for x in final:
                for head in range(heads):
                    piece = x[:, head * hd : (head + 1) * hd]
                    square += piece * piece
            scale = lax.rsqrt(jnp.sum(square, axis=-1, keepdims=True) / width + EPS)
            velocity = jnp.zeros((rows, latent_ref.shape[2]), F32)
            for at in everyone:
                normed = final[at] * scale * out_gain_ref[columns_of(at)][None, :]
                velocity += contract_last(normed.astype(BF), w_out_ref[:, columns_of(at)])
            sigma = [
                jnp.full((1, velocity.shape[1]), ts_ref[at], jnp.int32).astype(F32) / 1000.0
                for at in (0, 1)
            ]
            return latent_ref[patch] + (sigma[1] - sigma[0]) * velocity

        def send(block, job, distance):
            at = seen_as[distance]
            slot = job + jnp.where(last, jobs, 0) if block else job
            return pltpu.make_async_remote_copy(
                src_ref=sent.at[block, job],
                dst_ref=arrived.at[1 - block, slot, at],
                send_sem=sent_sem.at[block, job, distance],
                recv_sem=arrived_sem.at[1 - block, slot, at],
                device_id={
                    "pipe": onward if block else jnp.where(edge, 1, section),
                    "ulysses": peer(distance),
                },
                device_id_type=mesh_id,
            )

        def send_low(job):
            return pltpu.make_async_remote_copy(
                src_ref=sent_low.at[job],
                dst_ref=arrived_low.at[job],
                send_sem=sent_low_sem.at[job],
                recv_sem=low_sem.at[job],
                device_id={"pipe": jnp.where(edge, 1, onward)},
                device_id_type=mesh_id,
            )

        def run(block, step, patch):
            job = step * patches + patch
            gain = gains[block, step]
            if block == 0:

                @pl.when(edge & (step == 0))
                def _():
                    embed(job, latent_ref[patch])

                @pl.when(edge & (step > 0))
                def _():
                    embed(job, next_state(patch))

            else:

                @pl.when(first)
                def _():
                    receive(1, job, 0).wait()
                    receive_low(job).wait()
                    kept[patch] = arrived[1, job, 0].astype(F32) + arrived_low[job].astype(F32)

            square = jnp.zeros((rows, hd), F32)
            raw = None
            for at in everyone:
                if block == 0:

                    @pl.when(jnp.logical_not(edge))
                    def _():
                        receive(block, job, at).wait()

                elif at:
                    receive(block, job, at).wait()
                if at or block == 0:
                    x = arrived[block, job, at].astype(F32)
                else:
                    x = kept[patch]
                for head in range(heads):
                    piece = x[:, head * hd : (head + 1) * hd]
                    square += piece * piece
                x = (x * gain[:, at * slab : (at + 1) * slab]).astype(BF)
                term = jnp.dot(
                    x, w_ref[block, at * slab : (at + 1) * slab, :], preferred_element_type=F32
                )
                raw = term if raw is None else raw + term
            mean_square = jnp.sum(square, axis=-1, keepdims=True) / width
            scale = lax.rsqrt(mean_square + EPS)
            eps = EPS * (mean_square + EPS)

            def of(kind, head):
                column = (kind * heads + head) * hd
                return raw[:, column : column + hd]

            def head_scale(value):
                return lax.rsqrt(jnp.mean(value * value, axis=-1, keepdims=True) + eps)

            here = pl.ds(pl.multiple_of(patch * rows, rows), rows)
            for head in range(heads):
                columns = slice(head * hd, (head + 1) * hd)
                key = of(0, head)
                key = key * head_scale(key) * k_gain_ref[block]
                caches_ref[block, 0, here, columns] = key.astype(BF)
            for head in range(heads):
                columns = slice(head * hd, (head + 1) * hd)
                caches_ref[block, 1, here, columns] = (of(2, head) * scale).astype(BF)
            limit = jnp.where(step == 0, (patch + 1) * rows, tokens)
            allowed = lax.broadcasted_iota(jnp.int32, (rows, tokens), 1) < limit
            weights = []
            for head in range(heads):
                columns = slice(head * hd, (head + 1) * hd)
                query = of(1, head)
                scores = contract_last(
                    (query * q_gain_ref[block]).astype(BF), caches_ref[block, 0, :, columns]
                )
                scores = scores * (head_scale(query) * (hd**-0.5))
                weights.append(jnp.where(allowed, jnp.exp(scores), 0.0))
            if block == 0:

                @pl.when(jnp.logical_not(edge))
                def _():
                    receive_low(job).wait()

            for head in range(heads):
                columns = slice(head * hd, (head + 1) * hd)
                total = jnp.sum(weights[head], axis=-1, keepdims=True)
                attended = jnp.dot(
                    weights[head].astype(BF),
                    caches_ref[block, 1, :, columns],
                    preferred_element_type=F32,
                )
                attended = (attended / total).astype(BF).astype(F32)
                if block == 0:
                    x = arrived[0, job, 0, :, columns].astype(F32)
                    x = x + arrived_low[job, :, columns].astype(F32) + attended
                    kept[patch, :, columns] = x
                    sent[0, job, :, columns] = x.astype(BF)
                else:
                    x = kept[patch, :, columns] + attended
                    high = x.astype(BF)
                    sent[1, job, :, columns] = high
                    sent_low[job, :, columns] = (x - high.astype(F32)).astype(BF)

            if block == 0:
                for distance in distances[:0:-1]:
                    send(0, job, distance).start()

                @pl.when(edge)
                def _():
                    send(0, job, 0).start()
                    sent_low[job] = (kept[patch] - sent[0, job].astype(F32)).astype(BF)
                    send_low(job).start()

            else:

                @pl.when(jnp.logical_not(last) | (step < steps - 1))
                def _():
                    for distance in distances[::-1]:
                        send(1, job, distance).start()

                @pl.when(jnp.logical_not(last))
                def _():
                    send_low(job).start()

        turns = patches + 1

        def turn(at, _):
            step = at // turns
            patch = at - step * turns

            @pl.when((patch < patches) & leads)
            def _():
                run(0, step, patch)

            @pl.when((at == steps * turns - 1) & worker & jnp.logical_not(first))
            def _():
                hand_back().start()

            @pl.when((patch > 0) & worker)
            def _():
                run(1, step, patch - 1)

            return 0

        lax.fori_loop(0, steps * turns, turn, 0)
        def write_out(block):
            return pltpu.make_async_copy(caches_ref.at[block], out_hbm.at[0], out_sem)

        @pl.when(worker)
        def _():
            write_out(1).start()

        @pl.when(edge)
        def _():
            write_out(0).start()

        def finish(job, _):
            @pl.when(leads)
            def _():
                for distance in distances[1:]:
                    send(0, job, distance).wait_send()

            @pl.when(edge)
            def _():
                send(0, job, 0).wait_send()

            @pl.when(worker & (jnp.logical_not(last) | (job < jobs - patches)))
            def _():
                for distance in everyone:
                    send(1, job, distance).wait_send()

            @pl.when(edge | (worker & jnp.logical_not(last)))
            def _():
                send_low(job).wait_send()

            return 0

        lax.fori_loop(0, jobs, finish, 0)

        @pl.when(worker & jnp.logical_not(first))
        def _():
            hand_back().wait_send()

        write_out(0).wait()


def shards(latent, timesteps, w_in, w_out, out_gain, w_qkv, norm_gain, modulation, q_gain, k_gain):
    sections = lax.axis_size("pipe")
    groups = lax.axis_size("ulysses")
    patches, rows, channels = latent.shape
    steps = timesteps.shape[0]
    width = w_in.shape[1]
    heads, hd = w_qkv.shape[2], w_qkv.shape[4]
    jobs = steps * patches
    slab = heads * hd
    tokens = patches * rows
    dma = pltpu.SemaphoreType.DMA
    parameters = 4 + 3 * heads * groups
    return pl.pallas_call(
        functools.partial(pipeline, (sections, groups, steps, patches, rows, heads, hd)),
        out_shape=jax.ShapeDtypeStruct((1, 2, tokens, slab), BF),
        in_specs=[pl.BlockSpec(memory_space=pltpu.SMEM)] + [pl.BlockSpec(memory_space=pl.ANY)] * 9,
        out_specs=pl.BlockSpec(memory_space=pl.ANY),
        scratch_shapes=[
            pltpu.VMEM((patches, rows, channels), F32),
            pltpu.VMEM((channels, width), BF),
            pltpu.VMEM((channels, width), BF),
            pltpu.VMEM((width,), F32),
            pltpu.VMEM((2, 1, width), F32),
            pltpu.VMEM((2, 1, width), F32),
            pltpu.VMEM((2, 1, hd), F32),
            pltpu.VMEM((2, 1, hd), F32),
            pltpu.VMEM((2, width, 3 * slab), BF),
            pltpu.VMEM((2, steps, 1, width), F32),
            pltpu.VMEM((2, 2, tokens, slab), BF),
            pltpu.VMEM((2, jobs + patches, groups, rows, slab), BF),
            pltpu.VMEM((jobs, rows, slab), BF),
            pltpu.VMEM((patches, rows, slab), F32),
            pltpu.VMEM((2, jobs, rows, slab), BF),
            pltpu.VMEM((jobs, rows, slab), BF),
            dma((4,)),
            dma((2, parameters)),
            dma((parameters,)),
            dma((2, jobs + patches, groups)),
            dma((jobs,)),
            dma((2, jobs, groups)),
            dma((jobs,)),
            dma((2,)),
            dma,
        ],
        compiler_params=pltpu.CompilerParams(
            collective_id=0, has_side_effects=True, vmem_limit_bytes=60 << 20
        ),
        name="pipeline",
    )(
        timesteps,
        latent,
        w_in,
        w_out.T,
        out_gain,
        norm_gain,
        modulation,
        q_gain,
        k_gain,
        jnp.transpose(w_qkv, (0, 2, 3, 1, 4)),
    )


def solution(mesh):
    placed = (
        P("rep", None, None),
        P("rep"),
        P(),
        P(),
        P(),
        P("pipe", None, "ulysses", None, None),
        P("pipe", None),
        P("pipe", None),
        P("pipe", None),
        P("pipe", None),
    )
    return jax.shard_map(
        shards,
        mesh=mesh,
        in_specs=placed,
        out_specs=P("pipe", None, "rep", "ulysses"),
        check_vma=False,
    )
```

```python
import functools

import jax
import jax.numpy as jnp
from jax import lax
from jax.experimental import pallas as pl
from jax.experimental.pallas import tpu as pltpu
from jax.sharding import PartitionSpec as P

EPS = 1e-06
BF = jnp.bfloat16
F32 = jnp.float32


def contract_last(a, b):
    return lax.dot_general(a, b, (((1,), (1,)), ((), ())), preferred_element_type=F32)


def pipeline(
    dims,
    ts_ref,
    latent_hbm,
    w_in_hbm,
    w_out_hbm,
    out_gain_hbm,
    norm_gain_hbm,
    modulation_hbm,
    q_gain_hbm,
    k_gain_hbm,
    w_hbm,
    out_hbm,
    latent_ref,
    w_in_ref,
    w_out_ref,
    out_gain_ref,
    norm_gain_ref,
    modulation_ref,
    q_gain_ref,
    k_gain_ref,
    w_ref,
    gains,
    caches_ref,
    arrived,
    arrived_low,
    kept,
    sent,
    sent_low,
    edge_sem,
    w_sem,
    moved_sem,
    arrived_sem,
    low_sem,
    sent_sem,
    sent_low_sem,
    caches_sem,
    out_sem,
):
    sections, groups, steps, patches, rows, heads, hd = dims
    jobs = steps * patches
    slab = heads * hd
    width = groups * slab
    tokens = patches * rows
    section = lax.axis_index("pipe")
    member = lax.axis_index("ulysses")
    worker = lax.rem(section, 2) == 1
    helper = lax.rem(section, 2) == 0
    first = section < 2
    last = section >= sections - 2
    edge = section == 0
    following = lax.rem(section + 2, sections)
    preceding = lax.rem(section + sections - 2, sections)
    onward = jnp.where(last, 0, following)
    mesh_id = pl.DeviceIdType.MESH

    def peer(distance):
        return lax.rem(member + distance, groups)

    def greet(stage, distances):
        for distance in distances:
            pl.semaphore_signal(
                pltpu.get_barrier_semaphore(),
                inc=1,
                device_id={"pipe": stage, "ulysses": peer(distance)},
                device_id_type=mesh_id,
            )

    everyone = range(groups)

    @pl.when(helper & jnp.logical_not(edge))
    def _():
        greet(section + 1, [0])

    @pl.when(edge)
    def _():
        greet(sections - 1, everyone)
        greet(1, everyone)

    @pl.when(worker & first)
    def _():
        greet(0, everyone)

    @pl.when(worker & jnp.logical_not(first))
    def _():
        greet(section - 1, [0])
        greet(section, everyone[1:])
        greet(preceding, everyone)

    @pl.when(worker)
    def _():
        greet(onward, everyone)

    met = jnp.where(
        worker, jnp.where(first, 2 * groups, 3 * groups), jnp.where(edge, 2 * groups, 1)
    )
    leads = edge | (worker & jnp.logical_not(first))

    distances = sorted(everyone, key=lambda d: (min(d, groups - d), -d))
    batches = [[0, 1], list(range(2, groups))]
    seen_as = {d: distances.index((groups - d) % groups) for d in everyone}

    def columns_of(at):
        return pl.ds(pl.multiple_of(peer(distances[at]) * slab, slab), slab)

    pieces = [
        (norm_gain_hbm, norm_gain_ref),
        (modulation_hbm, modulation_ref),
        (q_gain_hbm, q_gain_ref),
        (k_gain_hbm, k_gain_ref),
    ]

    def parameter(block, at):
        if at < 4:
            return pieces[at][0], pieces[at][1].at[block]
        owner, matrix = divmod(at - 4, 3 * heads)
        kind, head = divmod(matrix, heads)
        column = matrix * hd
        return (
            w_hbm.at[0, head, (1, 0, 2)[kind], columns_of(owner)],
            w_ref.at[block, owner * slab : (owner + 1) * slab, column : column + hd],
        )

    parameters = range(4 + 3 * heads * groups)

    def load(at):
        return pltpu.make_async_copy(*parameter(1, at), w_sem.at[1, at])

    def hand(at):
        source, target = parameter(0, at)
        return pltpu.make_async_remote_copy(
            src_ref=source,
            dst_ref=target,
            send_sem=moved_sem.at[at],
            recv_sem=w_sem.at[0, at],
            device_id={"pipe": section + 1},
            device_id_type=mesh_id,
        )

    def handed(at):
        source, target = parameter(0, at)
        return pltpu.make_async_copy(source, target, w_sem.at[0, at])

    def hand_back():
        return pltpu.make_async_remote_copy(
            src_ref=caches_ref.at[0],
            dst_ref=caches_ref.at[0],
            send_sem=caches_sem.at[0],
            recv_sem=caches_sem.at[1],
            device_id={"pipe": section - 1},
            device_id_type=mesh_id,
        )

    def receive(block, job, at):
        slot = arrived.at[block, job, at]
        return pltpu.make_async_copy(slot, slot, arrived_sem.at[block, job, at])

    def receive_low(job):
        return pltpu.make_async_copy(sent_low.at[job], arrived_low.at[job], low_sem.at[job])

    @pl.when(helper & jnp.logical_not(edge))
    def _():
        pl.semaphore_wait(pltpu.get_barrier_semaphore(), met)
        for at in parameters:
            hand(at).start()
        for at in parameters:
            hand(at).wait_send()
        pltpu.make_async_copy(caches_ref.at[0], caches_ref.at[0], caches_sem.at[1]).wait()
        out = pltpu.make_async_copy(caches_ref.at[0], out_hbm.at[0], out_sem)
        out.start()
        out.wait()

    @pl.when(worker | edge)
    def _():
        first_only = [
            pltpu.make_async_copy(*pair, edge_sem.at[i])
            for i, pair in enumerate(
                [
                    (latent_hbm, latent_ref),
                    (w_in_hbm, w_in_ref),
                    (w_out_hbm, w_out_ref),
                    (out_gain_hbm, out_gain_ref),
                ]
            )
        ]

        @pl.when(edge)
        def _():
            for copy in first_only:
                copy.start()
            for at in parameters:
                handed(at).start()

        @pl.when(worker)
        def _():
            for at in parameters:
                load(at).start()

        caches_ref[...] = jnp.zeros_like(caches_ref)
        pl.semaphore_wait(pltpu.get_barrier_semaphore(), met)

        def prepare(block, copy):
            for at in range(4):
                copy(at).wait()
            for step in range(steps):
                sigma = jnp.full((1, slab), ts_ref[step], jnp.int32).astype(F32) / 1000.0
                for at in everyone:
                    gain = norm_gain_ref[block, :, columns_of(at)]
                    shift = modulation_ref[block, :, columns_of(at)]
                    gains[block, step, :, at * slab : (at + 1) * slab] = gain * (1.0 + sigma * shift)
            for at in parameters[4:]:
                copy(at).wait()

        @pl.when(edge)
        def _():
            for copy in first_only:
                copy.wait()

        @pl.when(leads)
        def _():
            prepare(0, handed)

        @pl.when(worker)
        def _():
            prepare(1, load)

        def embed(job, state):
            state = state.astype(BF)
            for at in everyone:
                x = jnp.dot(state, w_in_ref[:, columns_of(at)], preferred_element_type=F32)
                high = x.astype(BF)
                arrived[0, job, at] = high
                if at == 0:
                    arrived_low[job] = (x - high.astype(F32)).astype(BF)

        def next_state(patch):
            square = jnp.zeros((rows, hd), F32)
            for at in everyone:
                receive(0, jobs + patch, at).wait()
            final = [arrived[0, jobs + patch, at].astype(F32) for at in everyone]
            for x in final:
                for head in range(heads):
                    piece = x[:, head * hd : (head + 1) * hd]
                    square += piece * piece
            scale = lax.rsqrt(jnp.sum(square, axis=-1, keepdims=True) / width + EPS)
            velocity = jnp.zeros((rows, latent_ref.shape[2]), F32)
            for at in everyone:
                normed = final[at] * scale * out_gain_ref[columns_of(at)][None, :]
                velocity += contract_last(normed.astype(BF), w_out_ref[:, columns_of(at)])
            sigma = [
                jnp.full((1, velocity.shape[1]), ts_ref[at], jnp.int32).astype(F32) / 1000.0
                for at in (0, 1)
            ]
            return latent_ref[patch] + (sigma[1] - sigma[0]) * velocity

        def send(block, job, distance):
            at = seen_as[distance]
            slot = job + jnp.where(last, jobs, 0) if block else job
            return pltpu.make_async_remote_copy(
                src_ref=sent.at[block, job],
                dst_ref=arrived.at[1 - block, slot, at],
                send_sem=sent_sem.at[block, job, distance],
                recv_sem=arrived_sem.at[1 - block, slot, at],
                device_id={
                    "pipe": onward if block else jnp.where(edge, 1, section),
                    "ulysses": peer(distance),
                },
                device_id_type=mesh_id,
            )

        def send_low(job):
            return pltpu.make_async_remote_copy(
                src_ref=sent_low.at[job],
                dst_ref=arrived_low.at[job],
                send_sem=sent_low_sem.at[job],
                recv_sem=low_sem.at[job],
                device_id={"pipe": jnp.where(edge, 1, onward)},
                device_id_type=mesh_id,
            )

        def run(block, step, patch):
            job = step * patches + patch
            gain = gains[block, step]
            if block == 0:

                @pl.when(edge & (step == 0))
                def _():
                    embed(job, latent_ref[patch])

                @pl.when(edge & (step > 0))
                def _():
                    embed(job, next_state(patch))

            else:

                @pl.when(first)
                def _():
                    receive(1, job, 0).wait()
                    receive_low(job).wait()
                    kept[patch] = arrived[1, job, 0].astype(F32) + arrived_low[job].astype(F32)

            square = jnp.zeros((rows, hd), F32)
            raw, done = None, 0
            for owners in batches:
                if block == 0:

                    @pl.when(jnp.logical_not(edge))
                    def _():
                        for at in owners:
                            receive(block, job, at).wait()

                else:
                    for at in owners:
                        if at:
                            receive(block, job, at).wait()
                inputs = []
                for at in owners:
                    if at or block == 0:
                        x = arrived[block, job, at].astype(F32)
                    else:
                        x = kept[patch]
                    for head in range(heads):
                        piece = x[:, head * hd : (head + 1) * hd]
                        square += piece * piece
                    inputs.append((x * gain[:, at * slab : (at + 1) * slab]).astype(BF))
                depth = slice(done, done + len(owners) * slab)
                done = depth.stop
                term = jnp.dot(
                    jnp.concatenate(inputs, axis=1) if len(inputs) > 1 else inputs[0],
                    w_ref[block, depth, :],
                    preferred_element_type=F32,
                )
                raw = term if raw is None else raw + term
            mean_square = jnp.sum(square, axis=-1, keepdims=True) / width
            scale = lax.rsqrt(mean_square + EPS)
            eps = EPS * (mean_square + EPS)

            def of(kind, head):
                column = (kind * heads + head) * hd
                return raw[:, column : column + hd]

            def head_scale(value):
                return lax.rsqrt(jnp.mean(value * value, axis=-1, keepdims=True) + eps)

            here = pl.ds(pl.multiple_of(patch * rows, rows), rows)
            for head in range(heads):
                columns = slice(head * hd, (head + 1) * hd)
                key = of(0, head)
                key = key * head_scale(key) * k_gain_ref[block]
                caches_ref[block, 0, here, columns] = key.astype(BF)
            for head in range(heads):
                columns = slice(head * hd, (head + 1) * hd)
                caches_ref[block, 1, here, columns] = (of(2, head) * scale).astype(BF)
            limit = jnp.where(step == 0, (patch + 1) * rows, tokens)
            allowed = lax.broadcasted_iota(jnp.int32, (rows, tokens), 1) < limit
            weights = []
            for head in range(heads):
                columns = slice(head * hd, (head + 1) * hd)
                query = of(1, head)
                scores = contract_last(
                    (query * q_gain_ref[block]).astype(BF), caches_ref[block, 0, :, columns]
                )
                scores = scores * (head_scale(query) * (hd**-0.5))
                weights.append(jnp.where(allowed, jnp.exp(scores), 0.0))
            if block == 0:

                @pl.when(jnp.logical_not(edge))
                def _():
                    receive_low(job).wait()

            for head in range(heads):
                columns = slice(head * hd, (head + 1) * hd)
                total = jnp.sum(weights[head], axis=-1, keepdims=True)
                attended = jnp.dot(
                    weights[head].astype(BF),
                    caches_ref[block, 1, :, columns],
                    preferred_element_type=F32,
                )
                attended = (attended / total).astype(BF).astype(F32)
                if block == 0:
                    x = arrived[0, job, 0, :, columns].astype(F32)
                    x = x + arrived_low[job, :, columns].astype(F32) + attended
                    kept[patch, :, columns] = x
                    sent[0, job, :, columns] = x.astype(BF)
                else:
                    x = kept[patch, :, columns] + attended
                    high = x.astype(BF)
                    sent[1, job, :, columns] = high
                    sent_low[job, :, columns] = (x - high.astype(F32)).astype(BF)

            if block == 0:
                for distance in distances[:0:-1]:
                    send(0, job, distance).start()

                @pl.when(edge)
                def _():
                    send(0, job, 0).start()
                    sent_low[job] = (kept[patch] - sent[0, job].astype(F32)).astype(BF)
                    send_low(job).start()

            else:

                @pl.when(jnp.logical_not(last) | (step < steps - 1))
                def _():
                    for distance in distances[::-1]:
                        send(1, job, distance).start()

                @pl.when(jnp.logical_not(last))
                def _():
                    send_low(job).start()

        turns = patches + 1

        def turn(at, _):
            step = at // turns
            patch = at - step * turns

            @pl.when((patch < patches) & leads)
            def _():
                run(0, step, patch)

            @pl.when((at == steps * turns - 1) & worker & jnp.logical_not(first))
            def _():
                hand_back().start()

            @pl.when((patch > 0) & worker)
            def _():
                run(1, step, patch - 1)

            return 0

        lax.fori_loop(0, steps * turns, turn, 0)
        def write_out(block):
            return pltpu.make_async_copy(caches_ref.at[block], out_hbm.at[0], out_sem)

        @pl.when(worker)
        def _():
            write_out(1).start()

        @pl.when(edge)
        def _():
            write_out(0).start()

        def finish(job, _):
            @pl.when(leads)
            def _():
                for distance in distances[1:]:
                    send(0, job, distance).wait_send()

            @pl.when(edge)
            def _():
                send(0, job, 0).wait_send()

            @pl.when(worker & (jnp.logical_not(last) | (job < jobs - patches)))
            def _():
                for distance in everyone:
                    send(1, job, distance).wait_send()

            @pl.when(edge | (worker & jnp.logical_not(last)))
            def _():
                send_low(job).wait_send()

            return 0

        lax.fori_loop(0, jobs, finish, 0)

        @pl.when(worker & jnp.logical_not(first))
        def _():
            hand_back().wait_send()

        write_out(0).wait()


def shards(latent, timesteps, w_in, w_out, out_gain, w_qkv, norm_gain, modulation, q_gain, k_gain):
    sections = lax.axis_size("pipe")
    groups = lax.axis_size("ulysses")
    patches, rows, channels = latent.shape
    steps = timesteps.shape[0]
    width = w_in.shape[1]
    heads, hd = w_qkv.shape[2], w_qkv.shape[4]
    jobs = steps * patches
    slab = heads * hd
    tokens = patches * rows
    dma = pltpu.SemaphoreType.DMA
    parameters = 4 + 3 * heads * groups
    return pl.pallas_call(
        functools.partial(pipeline, (sections, groups, steps, patches, rows, heads, hd)),
        out_shape=jax.ShapeDtypeStruct((1, 2, tokens, slab), BF),
        in_specs=[pl.BlockSpec(memory_space=pltpu.SMEM)] + [pl.BlockSpec(memory_space=pl.ANY)] * 9,
        out_specs=pl.BlockSpec(memory_space=pl.ANY),
        scratch_shapes=[
            pltpu.VMEM((patches, rows, channels), F32),
            pltpu.VMEM((channels, width), BF),
            pltpu.VMEM((channels, width), BF),
            pltpu.VMEM((width,), F32),
            pltpu.VMEM((2, 1, width), F32),
            pltpu.VMEM((2, 1, width), F32),
            pltpu.VMEM((2, 1, hd), F32),
            pltpu.VMEM((2, 1, hd), F32),
            pltpu.VMEM((2, width, 3 * slab), BF),
            pltpu.VMEM((2, steps, 1, width), F32),
            pltpu.VMEM((2, 2, tokens, slab), BF),
            pltpu.VMEM((2, jobs + patches, groups, rows, slab), BF),
            pltpu.VMEM((jobs, rows, slab), BF),
            pltpu.VMEM((patches, rows, slab), F32),
            pltpu.VMEM((2, jobs, rows, slab), BF),
            pltpu.VMEM((jobs, rows, slab), BF),
            dma((4,)),
            dma((2, parameters)),
            dma((parameters,)),
            dma((2, jobs + patches, groups)),
            dma((jobs,)),
            dma((2, jobs, groups)),
            dma((jobs,)),
            dma((2,)),
            dma,
        ],
        compiler_params=pltpu.CompilerParams(
            collective_id=0, has_side_effects=True, vmem_limit_bytes=60 << 20
        ),
        name="pipeline",
    )(
        timesteps,
        latent,
        w_in,
        w_out.T,
        out_gain,
        norm_gain,
        modulation,
        q_gain,
        k_gain,
        jnp.transpose(w_qkv, (0, 2, 3, 1, 4)),
    )


def solution(mesh):
    placed = (
        P("rep", None, None),
        P("rep"),
        P(),
        P(),
        P(),
        P("pipe", None, "ulysses", None, None),
        P("pipe", None),
        P("pipe", None),
        P("pipe", None),
        P("pipe", None),
    )
    return jax.shard_map(
        shards,
        mesh=mesh,
        in_specs=placed,
        out_specs=P("pipe", None, "rep", "ulysses"),
        check_vma=False,
    )
```

```python
import functools

import jax
import jax.numpy as jnp
from jax import lax
from jax.experimental import pallas as pl
from jax.experimental.pallas import tpu as pltpu
from jax.sharding import PartitionSpec as P

EPS = 1e-06
BF = jnp.bfloat16
F32 = jnp.float32


def contract_last(a, b):
    return lax.dot_general(a, b, (((1,), (1,)), ((), ())), preferred_element_type=F32)


def pipeline(
    dims,
    ts_ref,
    latent_hbm,
    w_in_hbm,
    w_out_hbm,
    out_gain_hbm,
    norm_gain_hbm,
    modulation_hbm,
    q_gain_hbm,
    k_gain_hbm,
    w_hbm,
    out_hbm,
    latent_ref,
    w_in_ref,
    w_out_ref,
    out_gain_ref,
    norm_gain_ref,
    modulation_ref,
    q_gain_ref,
    k_gain_ref,
    w_ref,
    gains,
    caches_ref,
    arrived,
    arrived_low,
    kept,
    sent,
    sent_low,
    edge_sem,
    w_sem,
    moved_sem,
    arrived_sem,
    low_sem,
    sent_sem,
    sent_low_sem,
    caches_sem,
    out_sem,
):
    sections, groups, steps, patches, rows, heads, hd = dims
    jobs = steps * patches
    slab = heads * hd
    width = groups * slab
    tokens = patches * rows
    section = lax.axis_index("pipe")
    member = lax.axis_index("ulysses")
    worker = lax.rem(section, 2) == 1
    helper = lax.rem(section, 2) == 0
    first = section < 2
    last = section >= sections - 2
    edge = section == 0
    following = lax.rem(section + 2, sections)
    preceding = lax.rem(section + sections - 2, sections)
    onward = jnp.where(last, 0, following)
    mesh_id = pl.DeviceIdType.MESH

    def peer(distance):
        return lax.rem(member + distance, groups)

    def greet(stage, distances):
        for distance in distances:
            pl.semaphore_signal(
                pltpu.get_barrier_semaphore(),
                inc=1,
                device_id={"pipe": stage, "ulysses": peer(distance)},
                device_id_type=mesh_id,
            )

    everyone = range(groups)

    @pl.when(helper & jnp.logical_not(edge))
    def _():
        greet(section + 1, [0])

    @pl.when(edge)
    def _():
        greet(sections - 1, everyone)
        greet(1, everyone)

    @pl.when(worker & first)
    def _():
        greet(0, everyone)

    @pl.when(worker & jnp.logical_not(first))
    def _():
        greet(section - 1, [0])
        greet(section, everyone[1:])
        greet(preceding, everyone)

    @pl.when(worker)
    def _():
        greet(onward, everyone)

    met = jnp.where(
        worker, jnp.where(first, 2 * groups, 3 * groups), jnp.where(edge, 2 * groups, 1)
    )
    leads = edge | (worker & jnp.logical_not(first))

    distances = sorted(everyone, key=lambda d: (min(d, groups - d), -d))
    batches = [[0, 1], list(range(2, groups))]
    seen_as = {d: distances.index((groups - d) % groups) for d in everyone}

    def columns_of(at):
        return pl.ds(pl.multiple_of(peer(distances[at]) * slab, slab), slab)

    pieces = [
        (norm_gain_hbm, norm_gain_ref),
        (modulation_hbm, modulation_ref),
        (q_gain_hbm, q_gain_ref),
        (k_gain_hbm, k_gain_ref),
    ]

    def parameter(block, at):
        if at < 4:
            return pieces[at][0], pieces[at][1].at[block]
        owner, matrix = divmod(at - 4, 3 * heads)
        kind, head = divmod(matrix, heads)
        column = matrix * hd
        return (
            w_hbm.at[0, head, (1, 0, 2)[kind], columns_of(owner)],
            w_ref.at[block, owner * slab : (owner + 1) * slab, column : column + hd],
        )

    parameters = range(4 + 3 * heads * groups)

    def load(at):
        return pltpu.make_async_copy(*parameter(1, at), w_sem.at[1, at])

    def hand(at):
        source, target = parameter(0, at)
        return pltpu.make_async_remote_copy(
            src_ref=source,
            dst_ref=target,
            send_sem=moved_sem.at[at],
            recv_sem=w_sem.at[0, at],
            device_id={"pipe": section + 1},
            device_id_type=mesh_id,
        )

    def handed(at):
        source, target = parameter(0, at)
        return pltpu.make_async_copy(source, target, w_sem.at[0, at])

    def hand_back():
        return pltpu.make_async_remote_copy(
            src_ref=caches_ref.at[0],
            dst_ref=caches_ref.at[0],
            send_sem=caches_sem.at[0],
            recv_sem=caches_sem.at[1],
            device_id={"pipe": section - 1},
            device_id_type=mesh_id,
        )

    def receive(block, job, at):
        slot = arrived.at[block, job, at]
        return pltpu.make_async_copy(slot, slot, arrived_sem.at[block, job, at])

    def receive_low(job):
        return pltpu.make_async_copy(sent_low.at[job], arrived_low.at[job], low_sem.at[job])

    @pl.when(helper & jnp.logical_not(edge))
    def _():
        pl.semaphore_wait(pltpu.get_barrier_semaphore(), met)
        for at in parameters:
            hand(at).start()
        for at in parameters:
            hand(at).wait_send()
        pltpu.make_async_copy(caches_ref.at[0], caches_ref.at[0], caches_sem.at[1]).wait()
        out = pltpu.make_async_copy(caches_ref.at[0], out_hbm.at[0], out_sem.at[0])
        out.start()
        out.wait()

    @pl.when(worker | edge)
    def _():
        first_only = [
            pltpu.make_async_copy(*pair, edge_sem.at[i])
            for i, pair in enumerate(
                [
                    (latent_hbm, latent_ref),
                    (w_in_hbm, w_in_ref),
                    (w_out_hbm, w_out_ref),
                    (out_gain_hbm, out_gain_ref),
                ]
            )
        ]

        @pl.when(edge)
        def _():
            for copy in first_only:
                copy.start()
            for at in parameters:
                handed(at).start()

        @pl.when(worker)
        def _():
            for at in parameters:
                load(at).start()

        caches_ref[...] = jnp.zeros_like(caches_ref)
        pl.semaphore_wait(pltpu.get_barrier_semaphore(), met)

        def prepare(block, copy):
            for at in range(4):
                copy(at).wait()
            for step in range(steps):
                sigma = jnp.full((1, slab), ts_ref[step], jnp.int32).astype(F32) / 1000.0
                for at in everyone:
                    gain = norm_gain_ref[block, :, columns_of(at)]
                    shift = modulation_ref[block, :, columns_of(at)]
                    gains[block, step, :, at * slab : (at + 1) * slab] = gain * (1.0 + sigma * shift)
            for at in parameters[4:]:
                copy(at).wait()

        @pl.when(edge)
        def _():
            for copy in first_only:
                copy.wait()

        @pl.when(leads)
        def _():
            prepare(0, handed)

        @pl.when(worker)
        def _():
            prepare(1, load)

        def embed(job, state):
            state = state.astype(BF)
            for at in everyone:
                x = jnp.dot(state, w_in_ref[:, columns_of(at)], preferred_element_type=F32)
                high = x.astype(BF)
                arrived[0, job, at] = high
                if at == 0:
                    arrived_low[job] = (x - high.astype(F32)).astype(BF)

        def next_state(patch):
            square = jnp.zeros((rows, hd), F32)
            for at in everyone:
                receive(0, jobs + patch, at).wait()
            final = [arrived[0, jobs + patch, at].astype(F32) for at in everyone]
            for x in final:
                for head in range(heads):
                    piece = x[:, head * hd : (head + 1) * hd]
                    square += piece * piece
            scale = lax.rsqrt(jnp.sum(square, axis=-1, keepdims=True) / width + EPS)
            velocity = jnp.zeros((rows, latent_ref.shape[2]), F32)
            for at in everyone:
                normed = final[at] * scale * out_gain_ref[columns_of(at)][None, :]
                velocity += contract_last(normed.astype(BF), w_out_ref[:, columns_of(at)])
            sigma = [
                jnp.full((1, velocity.shape[1]), ts_ref[at], jnp.int32).astype(F32) / 1000.0
                for at in (0, 1)
            ]
            return latent_ref[patch] + (sigma[1] - sigma[0]) * velocity

        def send(block, job, distance):
            at = seen_as[distance]
            slot = job + jnp.where(last, jobs, 0) if block else job
            return pltpu.make_async_remote_copy(
                src_ref=sent.at[block, job],
                dst_ref=arrived.at[1 - block, slot, at],
                send_sem=sent_sem.at[block, job, distance],
                recv_sem=arrived_sem.at[1 - block, slot, at],
                device_id={
                    "pipe": onward if block else jnp.where(edge, 1, section),
                    "ulysses": peer(distance),
                },
                device_id_type=mesh_id,
            )

        def send_low(job):
            return pltpu.make_async_remote_copy(
                src_ref=sent_low.at[job],
                dst_ref=arrived_low.at[job],
                send_sem=sent_low_sem.at[job],
                recv_sem=low_sem.at[job],
                device_id={"pipe": jnp.where(edge, 1, onward)},
                device_id_type=mesh_id,
            )

        def run(block, step, patch):
            job = step * patches + patch
            gain = gains[block, step]
            if block == 0:

                @pl.when(edge & (step == 0))
                def _():
                    embed(job, latent_ref[patch])

                @pl.when(edge & (step > 0))
                def _():
                    embed(job, next_state(patch))

            else:

                @pl.when(first)
                def _():
                    receive(1, job, 0).wait()
                    receive_low(job).wait()
                    kept[patch] = arrived[1, job, 0].astype(F32) + arrived_low[job].astype(F32)

            square = jnp.zeros((rows, hd), F32)
            raw, done = None, 0
            for owners in batches:
                if block == 0:

                    @pl.when(jnp.logical_not(edge))
                    def _():
                        for at in owners:
                            receive(block, job, at).wait()

                else:
                    for at in owners:
                        if at:
                            receive(block, job, at).wait()
                inputs = []
                for at in owners:
                    if at or block == 0:
                        x = arrived[block, job, at].astype(F32)
                    else:
                        x = kept[patch]
                    for head in range(heads):
                        piece = x[:, head * hd : (head + 1) * hd]
                        square += piece * piece
                    inputs.append((x * gain[:, at * slab : (at + 1) * slab]).astype(BF))
                depth = slice(done, done + len(owners) * slab)
                done = depth.stop
                term = jnp.dot(
                    jnp.concatenate(inputs, axis=1) if len(inputs) > 1 else inputs[0],
                    w_ref[block, depth, :],
                    preferred_element_type=F32,
                )
                raw = term if raw is None else raw + term
            mean_square = jnp.sum(square, axis=-1, keepdims=True) / width
            scale = lax.rsqrt(mean_square + EPS)
            eps = EPS * (mean_square + EPS)

            def of(kind, head):
                column = (kind * heads + head) * hd
                return raw[:, column : column + hd]

            def head_scale(value):
                return lax.rsqrt(jnp.mean(value * value, axis=-1, keepdims=True) + eps)

            here = pl.ds(pl.multiple_of(patch * rows, rows), rows)
            for head in range(heads):
                columns = slice(head * hd, (head + 1) * hd)
                key = of(0, head)
                key = key * head_scale(key) * k_gain_ref[block]
                caches_ref[block, 0, here, columns] = key.astype(BF)
            for head in range(heads):
                columns = slice(head * hd, (head + 1) * hd)
                caches_ref[block, 1, here, columns] = (of(2, head) * scale).astype(BF)
            limit = jnp.where(step == 0, (patch + 1) * rows, tokens)
            allowed = lax.broadcasted_iota(jnp.int32, (rows, tokens), 1) < limit
            weights = []
            for head in range(heads):
                columns = slice(head * hd, (head + 1) * hd)
                query = of(1, head)
                scores = contract_last(
                    (query * q_gain_ref[block]).astype(BF), caches_ref[block, 0, :, columns]
                )
                scores = scores * (head_scale(query) * (hd**-0.5))
                weights.append(jnp.where(allowed, jnp.exp(scores), 0.0))
            if block == 0:

                @pl.when(jnp.logical_not(edge))
                def _():
                    receive_low(job).wait()

            for head in range(heads):
                columns = slice(head * hd, (head + 1) * hd)
                total = jnp.sum(weights[head], axis=-1, keepdims=True)
                attended = jnp.dot(
                    weights[head].astype(BF),
                    caches_ref[block, 1, :, columns],
                    preferred_element_type=F32,
                )
                attended = (attended / total).astype(BF).astype(F32)
                if block == 0:
                    x = arrived[0, job, 0, :, columns].astype(F32)
                    x = x + arrived_low[job, :, columns].astype(F32) + attended
                    kept[patch, :, columns] = x
                    sent[0, job, :, columns] = x.astype(BF)
                else:
                    x = kept[patch, :, columns] + attended
                    high = x.astype(BF)
                    sent[1, job, :, columns] = high
                    sent_low[job, :, columns] = (x - high.astype(F32)).astype(BF)

            if block == 0:
                for distance in distances[:0:-1]:
                    send(0, job, distance).start()

                @pl.when(edge)
                def _():
                    send(0, job, 0).start()
                    sent_low[job] = (kept[patch] - sent[0, job].astype(F32)).astype(BF)
                    send_low(job).start()

            else:

                @pl.when(jnp.logical_not(last) | (step < steps - 1))
                def _():
                    for distance in distances[::-1]:
                        send(1, job, distance).start()

                @pl.when(jnp.logical_not(last))
                def _():
                    send_low(job).start()

        def write_out(block, end):
            lines = pl.ds(tokens - rows, rows) if end else pl.ds(0, tokens - rows)
            return pltpu.make_async_copy(
                caches_ref.at[block, :, lines], out_hbm.at[0, :, lines], out_sem.at[end]
            )

        turns = patches + 1

        def turn(at, _):
            step = at // turns
            patch = at - step * turns

            @pl.when((patch < patches) & leads)
            def _():
                run(0, step, patch)

            @pl.when((at == steps * turns - 1) & worker & jnp.logical_not(first))
            def _():
                hand_back().start()

            @pl.when((at == steps * turns - 1) & worker)
            def _():
                write_out(1, 0).start()

            @pl.when((patch > 0) & worker)
            def _():
                run(1, step, patch - 1)

            return 0

        lax.fori_loop(0, steps * turns, turn, 0)
        @pl.when(worker)
        def _():
            write_out(1, 1).start()

        @pl.when(edge)
        def _():
            write_out(0, 0).start()
            write_out(0, 1).start()

        def finish(job, _):
            @pl.when(leads)
            def _():
                for distance in distances[1:]:
                    send(0, job, distance).wait_send()

            @pl.when(edge)
            def _():
                send(0, job, 0).wait_send()

            @pl.when(worker & (jnp.logical_not(last) | (job < jobs - patches)))
            def _():
                for distance in everyone:
                    send(1, job, distance).wait_send()

            @pl.when(edge | (worker & jnp.logical_not(last)))
            def _():
                send_low(job).wait_send()

            return 0

        lax.fori_loop(0, jobs, finish, 0)

        @pl.when(worker & jnp.logical_not(first))
        def _():
            hand_back().wait_send()

        write_out(0, 0).wait()
        write_out(0, 1).wait()


def shards(latent, timesteps, w_in, w_out, out_gain, w_qkv, norm_gain, modulation, q_gain, k_gain):
    sections = lax.axis_size("pipe")
    groups = lax.axis_size("ulysses")
    patches, rows, channels = latent.shape
    steps = timesteps.shape[0]
    width = w_in.shape[1]
    heads, hd = w_qkv.shape[2], w_qkv.shape[4]
    jobs = steps * patches
    slab = heads * hd
    tokens = patches * rows
    dma = pltpu.SemaphoreType.DMA
    parameters = 4 + 3 * heads * groups
    return pl.pallas_call(
        functools.partial(pipeline, (sections, groups, steps, patches, rows, heads, hd)),
        out_shape=jax.ShapeDtypeStruct((1, 2, tokens, slab), BF),
        in_specs=[pl.BlockSpec(memory_space=pltpu.SMEM)] + [pl.BlockSpec(memory_space=pl.ANY)] * 9,
        out_specs=pl.BlockSpec(memory_space=pl.ANY),
        scratch_shapes=[
            pltpu.VMEM((patches, rows, channels), F32),
            pltpu.VMEM((channels, width), BF),
            pltpu.VMEM((channels, width), BF),
            pltpu.VMEM((width,), F32),
            pltpu.VMEM((2, 1, width), F32),
            pltpu.VMEM((2, 1, width), F32),
            pltpu.VMEM((2, 1, hd), F32),
            pltpu.VMEM((2, 1, hd), F32),
            pltpu.VMEM((2, width, 3 * slab), BF),
            pltpu.VMEM((2, steps, 1, width), F32),
            pltpu.VMEM((2, 2, tokens, slab), BF),
            pltpu.VMEM((2, jobs + patches, groups, rows, slab), BF),
            pltpu.VMEM((jobs, rows, slab), BF),
            pltpu.VMEM((patches, rows, slab), F32),
            pltpu.VMEM((2, jobs, rows, slab), BF),
            pltpu.VMEM((jobs, rows, slab), BF),
            dma((4,)),
            dma((2, parameters)),
            dma((parameters,)),
            dma((2, jobs + patches, groups)),
            dma((jobs,)),
            dma((2, jobs, groups)),
            dma((jobs,)),
            dma((2,)),
            dma((2,)),
        ],
        compiler_params=pltpu.CompilerParams(
            collective_id=0, has_side_effects=True, vmem_limit_bytes=60 << 20
        ),
        name="pipeline",
    )(
        timesteps,
        latent,
        w_in,
        w_out.T,
        out_gain,
        norm_gain,
        modulation,
        q_gain,
        k_gain,
        jnp.transpose(w_qkv, (0, 2, 3, 1, 4)),
    )


def solution(mesh):
    placed = (
        P("rep", None, None),
        P("rep"),
        P(),
        P(),
        P(),
        P("pipe", None, "ulysses", None, None),
        P("pipe", None),
        P("pipe", None),
        P("pipe", None),
        P("pipe", None),
    )
    return jax.shard_map(
        shards,
        mesh=mesh,
        in_specs=placed,
        out_specs=P("pipe", None, "rep", "ulysses"),
        check_vma=False,
    )
```
